256 devices in a mesh: stream: 8 (over y, x_lo), tm: 32 (over x_hi, z, core).
Axes of the slice: x: 4 (x_hi: 2, x_lo: 2; x = x_hi * 2 + x_lo), y: 4, z: 8, core: 2. Of those that a mesh axis runs over, the one named last changes fastest.
Arguments:
- frames: bfloat16 [8, 16384, 1536], P('stream', 'tm')
- lengths: int32 [8], P('stream'), may hold values from 8192 to 16384, as said below
- attn_gain: float32 [1536], replicated, may hold values from 0.1 to 1.9
- w_qkv: bfloat16 [1536, 2304], P('stream', 'tm')
- w_out: bfloat16 [768, 1536], P('stream', 'tm'), may hold values from -0.75 to 0.75
- conv_gain: float32 [1536], replicated, may hold values from 0.1 to 1.9
- w_point_in: bfloat16 [1536, 3072], P('stream', 'tm'), may hold values from -0.15625 to 0.15625
- w_depth: float32 [31, 1536], replicated, may hold values from -1 to 1
- w_point_out: bfloat16 [1536, 1536], P('stream', 'tm'), may hold values from -0.15625 to 0.15625
Outputs:
- mixed: bfloat16 [8, 16384, 1536], P('stream', 'tm')
The draws below stay inside these ranges and needn't reach their ends.
Inputs may be any that keep to these rules, and one draw needn't show every extreme that they name: `lengths`: some stream has all 16384 frames valid and another exactly 8192.
All inputs are finite; a program needn't handle non-finite values.
Results may differ from the reference program's by a relative error of at most 0.0071.
Values may be sent and summed in bfloat16 or wider, within the bound.
No kernel may reach another device: no remote copies, remote signals or barrier semaphores. Data moves between devices by JAX's collectives and lax.ppermute only.
A program may use at most 128 MiB of HBM per device.

```python
import jax
import jax.numpy as jnp
from jax import lax

D = 1536
HEAD_DIM = 64
HEADS = 12
KERNEL = 31
WIN = 256
TOK_DEV = 512
STREAMS = 8
FRAMES = 16384


def draw_frames(key, part):
    key = jax.random.fold_in(key, 11)
    return jax.random.normal(key, (STREAMS, FRAMES, D), jnp.float32).astype(jnp.bfloat16)


def draw_lengths(key, part):
    key = jax.random.fold_in(key, 12)
    first_key, second_key, third_key = jax.random.split(key, 3)
    drawn = jax.random.randint(first_key, (STREAMS,), FRAMES // 2, FRAMES + 1)
    full = jax.random.randint(second_key, (), 0, STREAMS)
    other = (full + 1 + jax.random.randint(third_key, (), 0, STREAMS - 1)) % STREAMS
    slots = jnp.arange(STREAMS, dtype=jnp.int32)
    drawn = jnp.where(slots == full, FRAMES, drawn)
    drawn = jnp.where(slots == other, FRAMES // 2, drawn)
    return drawn.astype(jnp.int32)


def draw_w_qkv(key, part):
    key = jax.random.fold_in(key, 13)
    width = HEADS * HEAD_DIM
    return (jax.random.normal(key, (D, 3 * width), jnp.float32) / D ** 0.5).astype(jnp.bfloat16)


def block_scale(key, extent, cuts, least, largest):
    level = 1.0
    for axis_at, parts in cuts:
        heights = jax.random.uniform(jax.random.fold_in(jax.random.fold_in(key, 6), axis_at), (parts,), jnp.float32, least / len(cuts), largest / len(cuts))
        level = level * jnp.repeat(jnp.exp(heights), extent[axis_at] // parts).reshape((-1,) + (1,) * (len(extent) - 1 - axis_at))
    return level


def centred(stream_key, dims, scale, limit, cuts=(), kind=jnp.bfloat16):
    level = block_scale(stream_key, dims, cuts, -0.22, 0.18) if cuts else 1.0
    values = jax.random.normal(stream_key, dims, jnp.float32) * scale * level
    return jnp.minimum(jnp.maximum(values, -limit), limit).astype(kind)


def setup_inputs(seed: int = 0) -> dict:
    arg_keys = jax.random.split(jax.random.key(seed), 10)
    return {
        "frames": draw_frames(jax.random.fold_in(arg_keys[9], 71), 0),
        "lengths": draw_lengths(jax.random.fold_in(arg_keys[9], 71), 0),
        "attn_gain": jnp.clip(1.0 + 0.18 * jax.random.normal(arg_keys[2], (D,), jnp.float32), 0.1, 1.9),
        "w_qkv": draw_w_qkv(jax.random.fold_in(arg_keys[9], 71), 0),
        "w_out": centred(arg_keys[4], (HEADS * HEAD_DIM, D), HEAD_DIM ** -0.5, 0.75, ((0, 8), (1, 32))),
        "conv_gain": jnp.clip(1.0 + 0.18 * jax.random.normal(arg_keys[5], (D,), jnp.float32), 0.1, 1.9),
        "w_point_in": centred(arg_keys[6], (D, 2 * D), D ** -0.5, 0.15625, ((0, 8), (1, 32))),
        "w_depth": centred(arg_keys[7], (KERNEL, D), KERNEL ** -0.5, 1.0, (), jnp.float32),
        "w_point_out": centred(arg_keys[8], (D, D), D ** -0.5, 0.15625, ((0, 8), (1, 32))),
    }


def layer_norm(rows, gain):
    values = rows.astype(jnp.float32)
    center = values - lax.optimization_barrier(jnp.mean(values, axis=-1, keepdims=True))
    spread = lax.optimization_barrier(jnp.mean(center * center, axis=-1, keepdims=True))
    return center * lax.rsqrt(spread + 1e-05) * gain

def attend(q_block, kv_block, first, length):
    count = q_block.shape[0]
    span = kv_block.shape[0]
    reach = (span - count) // 2
    width = q_block.shape[1]
    query = q_block.reshape(count, -1, HEAD_DIM).astype(jnp.float32)
    keys = kv_block[:, :width].reshape(span, -1, HEAD_DIM).astype(jnp.float32)
    values = kv_block[:, width:].reshape(span, -1, HEAD_DIM).astype(jnp.float32)
    scores = jnp.einsum('ihd,jhd->hij', query, keys) * HEAD_DIM ** (-0.5)
    qpos = first + jnp.arange(count, dtype=jnp.int32)
    kpos = first - reach + jnp.arange(span, dtype=jnp.int32)
    allowed = (jnp.abs(qpos[:, None] - kpos[None, :]) <= reach) & (kpos[None, :] >= 0) & (kpos[None, :] < length)
    scores = jnp.where(allowed[None], scores, -1e+30)
    top = lax.optimization_barrier(jnp.max(scores, axis=-1, keepdims=True))
    expo = jnp.exp(scores - top)
    probs = (expo / lax.optimization_barrier(jnp.sum(expo, axis=-1, keepdims=True))).astype(jnp.bfloat16)
    context = jnp.einsum('hij,jhd->ihd', probs.astype(jnp.float32), values)
    return context.astype(jnp.bfloat16).reshape(count, width)

def reference(frames, lengths, attn_gain, w_qkv, w_out, conv_gain, w_point_in, w_depth, w_point_out):
    width = HEADS * HEAD_DIM
    half = KERNEL // 2

    def one_stream(item):
        rows, length = item
        total = rows.shape[0]
        normed = layer_norm(rows, attn_gain).astype(jnp.bfloat16)
        projected = jnp.dot(normed, w_qkv, preferred_element_type=jnp.float32).astype(jnp.bfloat16)
        query = projected[:, :width]
        padded = jnp.pad(projected[:, width:], ((WIN, WIN), (0, 0)))

        def one_block(block):
            first = (block * TOK_DEV).astype(jnp.int32)
            q_block = lax.dynamic_slice_in_dim(query, first, TOK_DEV, 0)
            kv_block = lax.dynamic_slice_in_dim(padded, first, TOK_DEV + 2 * WIN, 0)
            return attend(q_block, kv_block, first, length)
        context = lax.map(one_block, jnp.arange(total // TOK_DEV, dtype=jnp.int32)).reshape(total, width)
        after_attn = rows.astype(jnp.float32) + jnp.dot(context, w_out, preferred_element_type=jnp.float32)
        conv_in = layer_norm(after_attn, conv_gain).astype(jnp.bfloat16)
        glu = jnp.dot(conv_in, w_point_in, preferred_element_type=jnp.float32)
        valid = jnp.arange(total, dtype=jnp.int32) < length
        gated = jnp.where(valid[:, None], glu[:, :D] * jax.nn.sigmoid(glu[:, D:]), 0.0).astype(jnp.bfloat16)
        rimmed = jnp.pad(gated, ((half, half), (0, 0)))
        depth = jnp.zeros((total, D), jnp.float32)
        for tap in range(KERNEL):
            depth = depth + rimmed[tap:tap + total].astype(jnp.float32) * w_depth[tap]
        act = (depth * jax.nn.sigmoid(depth)).astype(jnp.bfloat16)
        result = after_attn + jnp.dot(act, w_point_out, preferred_element_type=jnp.float32)
        return jnp.where(valid[:, None], result, 0.0).astype(jnp.bfloat16)
    return lax.map(one_stream, (frames, lengths))
```

```python
import functools

import jax
import jax.numpy as jnp
from jax import lax
from jax.experimental import pallas as pl
from jax.experimental.pallas import tpu as pltpu
from jax.sharding import PartitionSpec as P

D = 1536
HEAD_DIM = 64
HEADS = 12
KERNEL = 31
WIN = 256
WIDTH = HEADS * HEAD_DIM

BOTH = ("stream", "tm")
PAD = 16
REACH = WIN + PAD
VMEM = 56 * 1024 * 1024


def place(x, y, z, core):
    return (2 * y + x % 2) * 32 + (x // 2) * 16 + 2 * z + core


CORE_SWAP = [(i, i ^ 1) for i in range(256)]
Z_GROUPS = [[hi * 16 + 2 * z + core for z in range(8)] for hi in range(2) for core in range(2)]
X_GROUPS = [
    [place(x, y, z, core) for x in range(4)]
    for y in range(4)
    for z in range(8)
    for core in range(2)
]


def shift(dx, dy):
    return [
        (place(x, y, z, core), place((x + dx) % 4, (y + dy) % 4, z, core))
        for x in range(4)
        for y in range(4)
        for z in range(8)
        for core in range(2)
    ]


def sent(block, way):
    return [block] + [lax.ppermute(block, BOTH, shift(d * way[0], d * way[1])) for d in (1, 2, 3)]


def in_order(parts, index, axis):
    back = jnp.flip(parts, axis)
    return lax.dynamic_slice_in_dim(jnp.concatenate([back, back], axis), 3 - index, 4, axis)


def layer_norm(rows, gain):
    values = rows.astype(jnp.float32)
    center = values - jnp.mean(values, axis=-1, keepdims=True)
    spread = jnp.mean(center * center, axis=-1, keepdims=True)
    return center * lax.rsqrt(spread + 1e-05) * gain


def exchange(block, axis, groups):
    count = len(groups[0])
    many = jnp.broadcast_to(block[None], (count,) + block.shape)
    return lax.all_to_all(many, axis, 0, 0, axis_index_groups=groups)


def project_kernel(pos_ref, before_ref, rows_ref, after_ref, gain_ref, *refs):
    sources, (q_ref, kv_ref, w_ref, x_ref, sem) = refs[:16], refs[16:]
    core, x, y = pos_ref[2], pos_ref[3], pos_ref[4]
    half = sources[0].shape[2]
    copies = []
    for number, src in enumerate(sources):
        by, cut, far = number // 8, number // 4 % 2, number % 4
        at = core if by == 0 else 1 - core
        for near in range(4):
            dx, dy = (near, far) if cut == 0 else (far, near)
            from_x = lax.rem(x + 4 - dx, 4)
            from_y = lax.rem(y + 4 - dy, 4)
            row = (from_y * 2 + lax.rem(from_x, 2)) * 192 + at * 96 + cut * 48
            copies.append(
                pltpu.make_async_copy(
                    src.at[near],
                    w_ref.at[
                        pl.ds(pl.multiple_of(row, 48), 48),
                        pl.ds(pl.multiple_of(from_x // 2 * half, half), half),
                    ],
                    sem.at[number * 4 + near],
                )
            )
    for copy in copies:
        copy.start()
    at = 0
    for part in (before_ref, rows_ref, after_ref):
        for row in range(0, part.shape[0], 16):
            x_ref[at : at + 16] = layer_norm(part[row : row + 16], gain_ref[...]).astype(
                jnp.bfloat16
            )
            at += 16
    for copy in copies:
        copy.wait()
    step = 256
    for n in range(0, WIDTH, step):
        q_ref[:, n : n + step] = jnp.dot(
            x_ref[WIN : WIN + q_ref.shape[0], :],
            w_ref[:, n : n + step],
            preferred_element_type=jnp.float32,
        ).astype(jnp.bfloat16)
    for n in range(WIDTH, 3 * WIDTH, step):
        kv_ref[:, n - WIDTH : n - WIDTH + step] = jnp.dot(
            x_ref[...], w_ref[:, n : n + step], preferred_element_type=jnp.float32
        ).astype(jnp.bfloat16)


def attend_kernel(pos_ref, q_ref, kv_ref, o_ref, cap_ref):
    first = pos_ref[0]
    length = pos_ref[1]
    blocks = [(0, 128), (128, 128), (256, 128), (384, 128), (512, 32)]
    for at, rows in blocks:
        span = rows + 2 * WIN
        i = lax.broadcasted_iota(jnp.int32, (rows, span), 0)
        j = lax.broadcasted_iota(jnp.int32, (rows, span), 1)
        kpos = first - REACH + at + j
        allowed = (j >= i) & (j <= i + 2 * WIN) & (kpos >= 0) & (kpos < length)
        cap_ref[pl.ds(at, rows), pl.ds(0, span)] = jnp.where(allowed, 3.0e38, -1e30)

    def pair(p, carry):
        lanes = pl.ds(pl.multiple_of(p * 128, 128), 128)
        vlanes = pl.ds(pl.multiple_of(WIDTH + p * 128, 128), 128)
        for at, rows in blocks:
            span = rows + 2 * WIN
            q = q_ref[pl.ds(at, rows), lanes] * jnp.bfloat16(0.125)
            k = kv_ref[pl.ds(at, span), lanes]
            v = kv_ref[pl.ds(at, span), vlanes]
            lane = lax.broadcasted_iota(jnp.int32, (rows, 128), 1)
            cap = cap_ref[pl.ds(at, rows), pl.ds(0, span)]
            wide = jnp.concatenate([v, jnp.ones((span, 128), jnp.bfloat16)], axis=1)
            both = jnp.concatenate(
                [
                    jnp.where(lane < 64, q, jnp.bfloat16(0)),
                    jnp.where(lane >= 64, q, jnp.bfloat16(0)),
                ],
                axis=0,
            )
            s = lax.dot_general(
                both, k, (((1,), (1,)), ((), ())), preferred_element_type=jnp.float32
            )
            s = jnp.minimum(s.reshape(2, rows, span), cap[None]).reshape(2 * rows, span)
            e = jnp.exp(s - jnp.max(s, axis=-1, keepdims=True)).astype(jnp.bfloat16)
            c = jnp.dot(e, wide, preferred_element_type=jnp.float32)
            c = c[:, :128] / c[:, 128:]
            parts = (c[:rows], c[rows:])
            o_ref[pl.ds(at, rows), lanes] = jnp.where(lane >= 64, parts[1], parts[0]).astype(
                jnp.bfloat16
            )
        return carry

    lax.fori_loop(0, HEADS // 2, pair, 0)


def middle_kernel(
    pos_ref, ctx_ref, before_ref, x_ref, behind_ref, gain_ref, taps_ref, mine_ref, other_ref,
    after_ref, act_ref, wo_ref, wi_ref, edge_ref, conv_ref, gated_a, gated_b, sem
):
    first = pos_ref[0]
    length = pos_ref[1]
    core = pos_ref[2]
    rows = ctx_ref.shape[0]
    count = after_ref.shape[0]
    out_copies, in_copies = [], []
    number = 0
    for src, at in ((mine_ref, core), (other_ref, 1 - core)):
        for z in range(8):
            for hi in range(2):
                to = pl.multiple_of(hi * 768 + z * 96 + at * 48, 48)
                out_copies.append(
                    pltpu.make_async_copy(
                        src.at[z, pl.ds(192, 48), pl.ds(hi * WIDTH, WIDTH)],
                        wo_ref.at[pl.ds(to, 48)],
                        sem.at[number],
                    )
                )
                to = pl.multiple_of(hi * 1536 + z * 192 + at * 96, 96)
                in_copies.append(
                    pltpu.make_async_copy(
                        src.at[z, pl.ds(hi * 96, 96)], wi_ref.at[pl.ds(to, 96)], sem.at[number + 1]
                    )
                )
                number += 2
    for copy in out_copies + in_copies:
        copy.start()

    nt = (((1,), (1,)), ((), ()))
    for copy in out_copies:
        copy.wait()
    for n in range(0, D, 256):
        added = lax.dot_general(
            ctx_ref[...], wo_ref[pl.ds(n, 256)], nt, preferred_element_type=jnp.float32
        )
        lane = slice(n, n + 256)
        edge = before_ref[REACH - PAD :, lane].astype(jnp.float32)
        edge_ref[:PAD, lane] = edge + added[:PAD]
        after_ref[:, lane] = x_ref[:, lane].astype(jnp.float32) + added[PAD : PAD + count]
        edge = behind_ref[:PAD, lane].astype(jnp.float32)
        edge_ref[PAD:, lane] = edge + added[PAD + count :]
    gain = gain_ref[...]
    conv_ref[:PAD] = layer_norm(edge_ref[:PAD], gain).astype(jnp.bfloat16)
    for at in range(0, count, 16):
        conv_ref[PAD + at : PAD + at + 16] = layer_norm(after_ref[at : at + 16], gain).astype(
            jnp.bfloat16
        )
    conv_ref[PAD + count :] = layer_norm(edge_ref[PAD:], gain).astype(jnp.bfloat16)
    for copy in in_copies:
        copy.wait()

    lanes = 256
    tile = 64
    index = first - PAD + lax.broadcasted_iota(jnp.int32, (rows, lanes), 0)
    valid = (index >= 0) & (index < length)

    buffers = (gated_a, gated_b)
    for step in range(D // lanes + 1):
        if step < D // lanes:
            to = step * lanes
            a = lax.dot_general(
                conv_ref[...], wi_ref[pl.ds(to, lanes)], nt, preferred_element_type=jnp.float32
            )
            b = lax.dot_general(
                conv_ref[...], wi_ref[pl.ds(to + D, lanes)], nt, preferred_element_type=jnp.float32
            )
            gated = jnp.where(valid, a * jax.nn.sigmoid(b), 0.0).astype(jnp.bfloat16)
            buffers[step % 2][...] = gated.astype(jnp.float32)
        if step == 0:
            continue
        to = (step - 1) * lanes
        gated_ref = buffers[(step - 1) % 2]
        for at in range(0, count, tile):
            depth = jnp.zeros((tile, lanes), jnp.float32)
            for r in range(8):
                steps = [o for o in range(r, 32, 8) if o >= 1]
                last = steps[-1] - r
                moved = gated_ref[at + r : at + r + tile + last, :]
                for o in steps:
                    weight = taps_ref[o - 1 : o, to : to + lanes]
                    depth = depth + moved[o - r : o - r + tile] * weight
            act_ref[at : at + tile, to : to + lanes] = (depth * jax.nn.sigmoid(depth)).astype(
                jnp.bfloat16
            )


def finish_kernel(pos_ref, after_ref, act_ref, mine_ref, other_ref, o_ref, w_ref, sem):
    count = o_ref.shape[0]
    core, y = pos_ref[2], pos_ref[4]
    copies = []
    for src, at in ((mine_ref, core), (other_ref, 1 - core)):
        for x in range(4):
            for dy in range(4):
                s = lax.rem(y + 4 - dy, 4) * 2 + x % 2
                for cut in range(2):
                    row = pl.multiple_of(s * 192 + at * 96 + cut * 48, 48)
                    copies.append(
                        pltpu.make_async_copy(
                            src.at[x, dy, :, pl.ds(cut * 768, 768)],
                            w_ref.at[pl.ds(row, 48), pl.ds(x // 2 * 768, 768)],
                            sem.at[len(copies)],
                        )
                    )
    for copy in copies:
        copy.start()
    for copy in copies:
        copy.wait()
    qpos = pos_ref[0] + lax.broadcasted_iota(jnp.int32, (count, 256), 0)
    keep = qpos < pos_ref[1]
    for n in range(0, D, 256):
        result = after_ref[:, n : n + 256] + jnp.dot(
            act_ref[...], w_ref[:, n : n + 256], preferred_element_type=jnp.float32
        )
        o_ref[:, n : n + 256] = jnp.where(keep, result, 0.0).astype(jnp.bfloat16)


SMEM_SPEC = pl.BlockSpec(memory_space=pltpu.SMEM)
VMEM_SPEC = pl.BlockSpec(memory_space=pltpu.VMEM)
ANY_SPEC = pl.BlockSpec(memory_space=pl.ANY)


def shards(frames, lengths, attn_gain, w_qkv, w_out, conv_gain, w_point_in, w_depth, w_point_out):
    rows = frames[0]
    count = rows.shape[0]
    tm = lax.axis_index("tm")
    core = tm % 2
    first = tm * count
    stream = lax.axis_index("stream")
    place_x, place_y = tm // 16 * 2 + stream % 2, stream // 2
    pos = jnp.stack([first, lengths[0], core, place_x, place_y]).astype(jnp.int32)

    up = [(s * 32 + i, s * 32 + i + 1) for s in range(8) for i in range(31)]
    down = [(j, i) for i, j in up]
    before = lax.ppermute(rows[count - REACH :], BOTH, up)
    after = lax.ppermute(rows[:REACH], BOTH, down)

    turned = jnp.concatenate(
        [w_point_in.T, jnp.concatenate([w_out.T[:24], w_out.T[24:]], axis=1)], axis=0
    )
    ys = jnp.stack(sent(turned, (0, 1)))

    pair = jnp.concatenate([w_qkv, w_point_out], axis=1)
    kept = lax.dynamic_slice_in_dim(pair, core * 96, 96, 0)
    given = lax.dynamic_slice_in_dim(pair, (1 - core) * 96, 96, 0)
    taken = lax.ppermute(given, BOTH, CORE_SWAP)
    even = jnp.where(core == 0, kept, taken)
    odd = jnp.where(core == 0, taken, kept)
    block = jnp.concatenate([even[:, :72], odd[:, :72], even[:, 72:], odd[:, 72:]], axis=1)
    column = exchange(block, "tm", Z_GROUPS)

    ys, before, after = lax.optimization_barrier((ys, before, after))
    xs = jnp.stack(sent(ys, (1, 0)))
    plane = in_order(in_order(xs, place_x, 0), place_y, 1)
    plane = plane.reshape(2, 2, 4, 120, 192)
    plane_in = plane[:, :, :, :96].transpose(0, 3, 2, 1, 4).reshape(192, D)
    plane_out = plane[:, :, :, 96:].reshape(2, 2, 4, 24, 2, 96)
    plane_out = plane_out.transpose(4, 3, 0, 2, 1, 5).reshape(48, D)
    line = jnp.concatenate([plane_in, plane_out], axis=0)
    column, line = lax.optimization_barrier((column, line))
    mid_mine = lax.all_gather(line, "tm", axis=0, tiled=False, axis_index_groups=Z_GROUPS)
    span = count + 2 * REACH
    inner = count + 2 * PAD

    q_column = column[:, :, :144].transpose(1, 0, 2).reshape(96, 1152)
    p_column = column[:, :, 144:].transpose(1, 0, 2).reshape(96, 768)
    xa = sent(q_column[:48], (1, 0))
    p_halves = jnp.concatenate([p_column[:48], p_column[48:]], axis=1)
    yb = jnp.stack(sent(jnp.concatenate([q_column[48:], p_halves], axis=1), (0, 1)))
    qkv_mine = sent(jnp.stack(xa), (0, 1)) + sent(yb[:, :, : 3 * WIDTH // 2], (1, 0))
    qkv_other = [lax.ppermute(part, BOTH, CORE_SWAP) for part in qkv_mine]
    tail = yb[:, :, 3 * WIDTH // 2 :]
    tail_mine = lax.all_gather(tail, BOTH, axis=0, tiled=False, axis_index_groups=X_GROUPS)

    q, kv = pl.pallas_call(
        project_kernel,
        out_shape=[
            jax.ShapeDtypeStruct((inner, WIDTH), jnp.bfloat16),
            jax.ShapeDtypeStruct((span, 2 * WIDTH), jnp.bfloat16),
        ],
        in_specs=[SMEM_SPEC] + [VMEM_SPEC] * 4 + [ANY_SPEC] * 16,
        out_specs=[VMEM_SPEC, VMEM_SPEC],
        scratch_shapes=[
            pltpu.VMEM((D, 3 * WIDTH), jnp.bfloat16),
            pltpu.VMEM((span, D), jnp.bfloat16),
            pltpu.SemaphoreType.DMA((64,)),
        ],
        compiler_params=pltpu.CompilerParams(vmem_limit_bytes=VMEM),
        cost_estimate=pl.CostEstimate(
            flops=2 * span * D * 3 * WIDTH, bytes_accessed=16 * 2**20, transcendentals=0
        ),
    )(pos, before, rows, after, attn_gain[None], *qkv_mine, *qkv_other)

    mid_mine, q, kv = lax.optimization_barrier((mid_mine, q, kv))
    mid_other = lax.ppermute(mid_mine, BOTH, CORE_SWAP)
    context = pl.pallas_call(
        attend_kernel,
        out_shape=jax.ShapeDtypeStruct((inner, WIDTH), jnp.bfloat16),
        in_specs=[SMEM_SPEC, VMEM_SPEC, VMEM_SPEC],
        out_specs=VMEM_SPEC,
        scratch_shapes=[pltpu.VMEM((inner, 128 + 2 * WIN), jnp.float32)],
        compiler_params=pltpu.CompilerParams(vmem_limit_bytes=VMEM),
        cost_estimate=pl.CostEstimate(
            flops=12 * 10**9, bytes_accessed=6 * 2**20, transcendentals=4 * 10**6
        ),
    )(pos, q, kv)

    after_attn, act = pl.pallas_call(
        middle_kernel,
        out_shape=[
            jax.ShapeDtypeStruct((count, D), jnp.float32),
            jax.ShapeDtypeStruct((count, D), jnp.bfloat16),
        ],
        in_specs=[SMEM_SPEC] + [VMEM_SPEC] * 6 + [ANY_SPEC] * 2,
        out_specs=[VMEM_SPEC, VMEM_SPEC],
        scratch_shapes=[
            pltpu.VMEM((D, WIDTH), jnp.bfloat16),
            pltpu.VMEM((2 * D, D), jnp.bfloat16),
            pltpu.VMEM((2 * PAD, D), jnp.float32),
            pltpu.VMEM((inner, D), jnp.bfloat16),
            pltpu.VMEM((inner, 256), jnp.float32),
            pltpu.VMEM((inner, 256), jnp.float32),
            pltpu.SemaphoreType.DMA((64,)),
        ],
        compiler_params=pltpu.CompilerParams(vmem_limit_bytes=VMEM),
        cost_estimate=pl.CostEstimate(
            flops=20 * 10**9, bytes_accessed=20 * 2**20, transcendentals=2 * 10**6
        ),
    )(
        pos,
        context,
        before,
        rows,
        after,
        conv_gain[None],
        w_depth,
        mid_mine,
        mid_other,
    )
    tail_mine, after_attn, act = lax.optimization_barrier((tail_mine, after_attn, act))
    tail_other = lax.ppermute(tail_mine, BOTH, CORE_SWAP)
    result = pl.pallas_call(
        finish_kernel,
        out_shape=jax.ShapeDtypeStruct((count, D), jnp.bfloat16),
        in_specs=[SMEM_SPEC] + [VMEM_SPEC] * 2 + [ANY_SPEC] * 2,
        out_specs=VMEM_SPEC,
        scratch_shapes=[pltpu.VMEM((D, D), jnp.bfloat16), pltpu.SemaphoreType.DMA((64,))],
        compiler_params=pltpu.CompilerParams(vmem_limit_bytes=VMEM),
        cost_estimate=pl.CostEstimate(
            flops=3 * 10**9, bytes_accessed=10 * 2**20, transcendentals=0
        ),
    )(pos, after_attn, act, tail_mine, tail_other)
    return result[None]


def solution(mesh):
    placed = (
        P("stream", "tm", None),
        P("stream"),
        P(),
        P("stream", "tm"),
        P("stream", "tm"),
        P(),
        P("stream", "tm"),
        P(),
        P("stream", "tm"),
    )
    return jax.shard_map(
        shards, mesh=mesh, in_specs=placed, out_specs=P("stream", "tm", None), check_vma=False
    )
```

```python
import functools

import jax
import jax.numpy as jnp
from jax import lax
from jax.experimental import pallas as pl
from jax.experimental.pallas import tpu as pltpu
from jax.sharding import PartitionSpec as P

D = 1536
HEAD_DIM = 64
HEADS = 12
KERNEL = 31
WIN = 256
WIDTH = HEADS * HEAD_DIM

BOTH = ("stream", "tm")
PAD = 16
REACH = WIN + PAD
VMEM = 56 * 1024 * 1024


def place(x, y, z, core):
    return (2 * y + x % 2) * 32 + (x // 2) * 16 + 2 * z + core


CORE_SWAP = [(i, i ^ 1) for i in range(256)]
Z_GROUPS = [[hi * 16 + 2 * z + core for z in range(8)] for hi in range(2) for core in range(2)]
X_GROUPS = [
    [place(x, y, z, core) for x in range(4)]
    for y in range(4)
    for z in range(8)
    for core in range(2)
]


def shift(dx, dy):
    return [
        (place(x, y, z, core), place((x + dx) % 4, (y + dy) % 4, z, core))
        for x in range(4)
        for y in range(4)
        for z in range(8)
        for core in range(2)
    ]


def sent(block, way):
    return [block] + [lax.ppermute(block, BOTH, shift(d * way[0], d * way[1])) for d in (1, 2, 3)]


def in_order(parts, index, axis):
    back = jnp.flip(parts, axis)
    return lax.dynamic_slice_in_dim(jnp.concatenate([back, back], axis), 3 - index, 4, axis)


def layer_norm(rows, gain):
    values = rows.astype(jnp.float32)
    center = values - jnp.mean(values, axis=-1, keepdims=True)
    spread = jnp.mean(center * center, axis=-1, keepdims=True)
    return center * lax.rsqrt(spread + 1e-05) * gain


def exchange(block, axis, groups):
    count = len(groups[0])
    many = jnp.broadcast_to(block[None], (count,) + block.shape)
    return lax.all_to_all(many, axis, 0, 0, axis_index_groups=groups)


def project_kernel(pos_ref, before_ref, rows_ref, after_ref, gain_ref, *refs):
    sources, (q_ref, kv_ref, w_ref, x_ref, sem) = refs[:16], refs[16:]
    core, x, y = pos_ref[2], pos_ref[3], pos_ref[4]
    half = sources[0].shape[2]
    copies = []
    for number, src in enumerate(sources):
        by, cut, far = number // 8, number // 4 % 2, number % 4
        at = core if by == 0 else 1 - core
        for near in range(4):
            dx, dy = (near, far) if cut == 0 else (far, near)
            from_x = lax.rem(x + 4 - dx, 4)
            from_y = lax.rem(y + 4 - dy, 4)
            row = (from_y * 2 + lax.rem(from_x, 2)) * 192 + at * 96 + cut * 48
            copies.append(
                pltpu.make_async_copy(
                    src.at[near],
                    w_ref.at[
                        pl.ds(pl.multiple_of(row, 48), 48),
                        pl.ds(pl.multiple_of(from_x // 2 * half, half), half),
                    ],
                    sem.at[number * 4 + near],
                )
            )
    for copy in copies:
        copy.start()
    at = 0
    for part in (before_ref, rows_ref, after_ref):
        for row in range(0, part.shape[0], 16):
            x_ref[at : at + 16] = layer_norm(part[row : row + 16], gain_ref[...]).astype(
                jnp.bfloat16
            )
            at += 16
    for copy in copies:
        copy.wait()
    step = 256
    for n in range(0, WIDTH, step):
        q_ref[:, n : n + step] = jnp.dot(
            x_ref[WIN : WIN + q_ref.shape[0], :],
            w_ref[:, n : n + step],
            preferred_element_type=jnp.float32,
        ).astype(jnp.bfloat16)
    for n in range(WIDTH, 3 * WIDTH, step):
        kv_ref[:, n - WIDTH : n - WIDTH + step] = jnp.dot(
            x_ref[...], w_ref[:, n : n + step], preferred_element_type=jnp.float32
        ).astype(jnp.bfloat16)


def attend_kernel(pos_ref, q_ref, kv_ref, o_ref, cap_ref):
    first = pos_ref[0]
    length = pos_ref[1]
    blocks = [(0, 128), (128, 128), (256, 128), (384, 128), (512, 32)]
    for at, rows in blocks:
        span = rows + 2 * WIN
        i = lax.broadcasted_iota(jnp.int32, (rows, span), 0)
        j = lax.broadcasted_iota(jnp.int32, (rows, span), 1)
        kpos = first - REACH + at + j
        allowed = (j >= i) & (j <= i + 2 * WIN) & (kpos >= 0) & (kpos < length)
        cap_ref[pl.ds(at, rows), pl.ds(0, span)] = jnp.where(allowed, 3.0e38, -1e30)

    def pair(p, carry):
        lanes = pl.ds(pl.multiple_of(p * 128, 128), 128)
        vlanes = pl.ds(pl.multiple_of(WIDTH + p * 128, 128), 128)
        for at, rows in blocks:
            span = rows + 2 * WIN
            q = q_ref[pl.ds(at, rows), lanes] * jnp.bfloat16(0.125)
            k = kv_ref[pl.ds(at, span), lanes]
            v = kv_ref[pl.ds(at, span), vlanes]
            lane = lax.broadcasted_iota(jnp.int32, (rows, 128), 1)
            cap = cap_ref[pl.ds(at, rows), pl.ds(0, span)]
            wide = jnp.concatenate([v, jnp.ones((span, 128), jnp.bfloat16)], axis=1)
            both = jnp.concatenate(
                [
                    jnp.where(lane < 64, q, jnp.bfloat16(0)),
                    jnp.where(lane >= 64, q, jnp.bfloat16(0)),
                ],
                axis=0,
            )
            s = lax.dot_general(
                both, k, (((1,), (1,)), ((), ())), preferred_element_type=jnp.float32
            )
            s = jnp.minimum(s.reshape(2, rows, span), cap[None]).reshape(2 * rows, span)
            e = jnp.exp(s - jnp.max(s, axis=-1, keepdims=True)).astype(jnp.bfloat16)
            c = jnp.dot(e, wide, preferred_element_type=jnp.float32)
            c = c[:, :128] / c[:, 128:]
            parts = (c[:rows], c[rows:])
            o_ref[pl.ds(at, rows), lanes] = jnp.where(lane >= 64, parts[1], parts[0]).astype(
                jnp.bfloat16
            )
        return carry

    lax.fori_loop(0, HEADS // 2, pair, 0, unroll=6)


def middle_kernel(
    pos_ref, ctx_ref, before_ref, x_ref, behind_ref, gain_ref, taps_ref, mine_ref, other_ref,
    after_ref, act_ref, wo_ref, wi_ref, edge_ref, conv_ref, gated_a, gated_b, sem
):
    first = pos_ref[0]
    length = pos_ref[1]
    core = pos_ref[2]
    rows = ctx_ref.shape[0]
    count = after_ref.shape[0]
    out_copies, in_copies = [], []
    number = 0
    for src, at in ((mine_ref, core), (other_ref, 1 - core)):
        for z in range(8):
            for hi in range(2):
                to = pl.multiple_of(hi * 768 + z * 96 + at * 48, 48)
                out_copies.append(
                    pltpu.make_async_copy(
                        src.at[z, pl.ds(192, 48), pl.ds(hi * WIDTH, WIDTH)],
                        wo_ref.at[pl.ds(to, 48)],
                        sem.at[number],
                    )
                )
                to = pl.multiple_of(hi * 1536 + z * 192 + at * 96, 96)
                in_copies.append(
                    pltpu.make_async_copy(
                        src.at[z, pl.ds(hi * 96, 96)], wi_ref.at[pl.ds(to, 96)], sem.at[number + 1]
                    )
                )
                number += 2
    for copy in out_copies + in_copies:
        copy.start()

    nt = (((1,), (1,)), ((), ()))
    for copy in out_copies:
        copy.wait()
    for n in range(0, D, 256):
        added = lax.dot_general(
            ctx_ref[...], wo_ref[pl.ds(n, 256)], nt, preferred_element_type=jnp.float32
        )
        lane = slice(n, n + 256)
        edge = before_ref[REACH - PAD :, lane].astype(jnp.float32)
        edge_ref[:PAD, lane] = edge + added[:PAD]
        after_ref[:, lane] = x_ref[:, lane].astype(jnp.float32) + added[PAD : PAD + count]
        edge = behind_ref[:PAD, lane].astype(jnp.float32)
        edge_ref[PAD:, lane] = edge + added[PAD + count :]
    gain = gain_ref[...]
    conv_ref[:PAD] = layer_norm(edge_ref[:PAD], gain).astype(jnp.bfloat16)
    for at in range(0, count, 16):
        conv_ref[PAD + at : PAD + at + 16] = layer_norm(after_ref[at : at + 16], gain).astype(
            jnp.bfloat16
        )
    conv_ref[PAD + count :] = layer_norm(edge_ref[PAD:], gain).astype(jnp.bfloat16)
    for copy in in_copies:
        copy.wait()

    lanes = 256
    tile = 64
    index = first - PAD + lax.broadcasted_iota(jnp.int32, (rows, lanes), 0)
    valid = (index >= 0) & (index < length)

    buffers = (gated_a, gated_b)
    for step in range(D // lanes + 1):
        if step < D // lanes:
            to = step * lanes
            a = lax.dot_general(
                conv_ref[...], wi_ref[pl.ds(to, lanes)], nt, preferred_element_type=jnp.float32
            )
            b = lax.dot_general(
                conv_ref[...], wi_ref[pl.ds(to + D, lanes)], nt, preferred_element_type=jnp.float32
            )
            gated = jnp.where(valid, a * jax.nn.sigmoid(b), 0.0).astype(jnp.bfloat16)
            buffers[step % 2][...] = gated.astype(jnp.float32)
        if step == 0:
            continue
        to = (step - 1) * lanes
        gated_ref = buffers[(step - 1) % 2]
        for at in range(0, count, tile):
            depth = jnp.zeros((tile, lanes), jnp.float32)
            for r in range(8):
                steps = [o for o in range(r, 32, 8) if o >= 1]
                last = steps[-1] - r
                moved = gated_ref[at + r : at + r + tile + last, :]
                for o in steps:
                    weight = taps_ref[o - 1 : o, to : to + lanes]
                    depth = depth + moved[o - r : o - r + tile] * weight
            act_ref[at : at + tile, to : to + lanes] = (depth * jax.nn.sigmoid(depth)).astype(
                jnp.bfloat16
            )


def finish_kernel(
    pos_ref, after_in, act_in, mine_ref, other_ref, o_ref, w_ref, after_ref, act_ref, sem
):
    count = o_ref.shape[0]
    core, y = pos_ref[2], pos_ref[4]
    copies = [
        pltpu.make_async_copy(act_in, act_ref, sem.at[64]),
        pltpu.make_async_copy(after_in, after_ref, sem.at[65]),
    ]
    for x in range(4):
        for src, at in ((mine_ref, core), (other_ref, 1 - core)):
            for dy in range(4):
                s = lax.rem(y + 4 - dy, 4) * 2 + x % 2
                for cut in range(2):
                    row = pl.multiple_of(s * 192 + at * 96 + cut * 48, 48)
                    copies.append(
                        pltpu.make_async_copy(
                            src.at[x, dy, :, pl.ds(cut * 768, 768)],
                            w_ref.at[pl.ds(row, 48), pl.ds(x // 2 * 768, 768)],
                            sem.at[len(copies) - 2],
                        )
                    )
    for copy in copies:
        copy.start()
    qpos = pos_ref[0] + lax.broadcasted_iota(jnp.int32, (count, 256), 0)
    keep = qpos < pos_ref[1]
    for hi in range(2):
        for copy in copies[34:] if hi else copies[:34]:
            copy.wait()
        for n in range(hi * 768, hi * 768 + 768, 256):
            result = after_ref[:, n : n + 256] + jnp.dot(
                act_ref[...], w_ref[:, n : n + 256], preferred_element_type=jnp.float32
            )
            o_ref[:, n : n + 256] = jnp.where(keep, result, 0.0).astype(jnp.bfloat16)


SMEM_SPEC = pl.BlockSpec(memory_space=pltpu.SMEM)
VMEM_SPEC = pl.BlockSpec(memory_space=pltpu.VMEM)
ANY_SPEC = pl.BlockSpec(memory_space=pl.ANY)


def shards(frames, lengths, attn_gain, w_qkv, w_out, conv_gain, w_point_in, w_depth, w_point_out):
    rows = frames[0]
    count = rows.shape[0]
    tm = lax.axis_index("tm")
    core = tm % 2
    first = tm * count
    stream = lax.axis_index("stream")
    place_x, place_y = tm // 16 * 2 + stream % 2, stream // 2
    pos = jnp.stack([first, lengths[0], core, place_x, place_y]).astype(jnp.int32)

    up = [(s * 32 + i, s * 32 + i + 1) for s in range(8) for i in range(31)]
    down = [(j, i) for i, j in up]
    before = lax.ppermute(rows[count - REACH :], BOTH, up)
    after = lax.ppermute(rows[:REACH], BOTH, down)

    turned = jnp.concatenate(
        [w_point_in.T, jnp.concatenate([w_out.T[:24], w_out.T[24:]], axis=1)], axis=0
    )
    ys = jnp.stack(sent(turned, (0, 1)))

    pair = jnp.concatenate([w_qkv, w_point_out], axis=1)
    kept = lax.dynamic_slice_in_dim(pair, core * 96, 96, 0)
    given = lax.dynamic_slice_in_dim(pair, (1 - core) * 96, 96, 0)
    taken = lax.ppermute(given, BOTH, CORE_SWAP)
    even = jnp.where(core == 0, kept, taken)
    odd = jnp.where(core == 0, taken, kept)
    block = jnp.concatenate([even[:, :72], odd[:, :72], even[:, 72:], odd[:, 72:]], axis=1)
    column = exchange(block, "tm", Z_GROUPS)

    ys, before, after = lax.optimization_barrier((ys, before, after))
    xs = jnp.stack(sent(ys, (1, 0)))
    plane = in_order(in_order(xs, place_x, 0), place_y, 1)
    plane = plane.reshape(2, 2, 4, 120, 192)
    plane_in = plane[:, :, :, :96].transpose(0, 3, 2, 1, 4).reshape(192, D)
    plane_out = plane[:, :, :, 96:].reshape(2, 2, 4, 24, 2, 96)
    plane_out = plane_out.transpose(4, 3, 0, 2, 1, 5).reshape(48, D)
    line = jnp.concatenate([plane_in, plane_out], axis=0)
    column, line = lax.optimization_barrier((column, line))
    mid_mine = lax.all_gather(line, "tm", axis=0, tiled=False, axis_index_groups=Z_GROUPS)
    span = count + 2 * REACH
    inner = count + 2 * PAD

    q_column = column[:, :, :144].transpose(1, 0, 2).reshape(96, 1152)
    p_column = column[:, :, 144:].transpose(1, 0, 2).reshape(96, 768)
    xa = sent(q_column[:48], (1, 0))
    p_halves = jnp.concatenate([p_column[:48], p_column[48:]], axis=1)
    yb = jnp.stack(sent(jnp.concatenate([q_column[48:], p_halves], axis=1), (0, 1)))
    qkv_mine = sent(jnp.stack(xa), (0, 1)) + sent(yb[:, :, : 3 * WIDTH // 2], (1, 0))
    qkv_mine = lax.optimization_barrier(qkv_mine)
    qkv_other = [lax.ppermute(part, BOTH, CORE_SWAP) for part in qkv_mine]
    tail = yb[:, :, 3 * WIDTH // 2 :]
    tail_mine = lax.all_gather(tail, BOTH, axis=0, tiled=False, axis_index_groups=X_GROUPS)

    q, kv = pl.pallas_call(
        project_kernel,
        out_shape=[
            jax.ShapeDtypeStruct((inner, WIDTH), jnp.bfloat16),
            jax.ShapeDtypeStruct((span, 2 * WIDTH), jnp.bfloat16),
        ],
        in_specs=[SMEM_SPEC] + [VMEM_SPEC] * 4 + [ANY_SPEC] * 16,
        out_specs=[VMEM_SPEC, VMEM_SPEC],
        scratch_shapes=[
            pltpu.VMEM((D, 3 * WIDTH), jnp.bfloat16),
            pltpu.VMEM((span, D), jnp.bfloat16),
            pltpu.SemaphoreType.DMA((64,)),
        ],
        compiler_params=pltpu.CompilerParams(vmem_limit_bytes=VMEM),
        cost_estimate=pl.CostEstimate(
            flops=2 * span * D * 3 * WIDTH, bytes_accessed=16 * 2**20, transcendentals=0
        ),
    )(pos, before, rows, after, attn_gain[None], *qkv_mine, *qkv_other)

    mid_mine, q, kv = lax.optimization_barrier((mid_mine, q, kv))
    mid_other = lax.ppermute(mid_mine, BOTH, CORE_SWAP)
    context = pl.pallas_call(
        attend_kernel,
        out_shape=jax.ShapeDtypeStruct((inner, WIDTH), jnp.bfloat16),
        in_specs=[SMEM_SPEC, VMEM_SPEC, VMEM_SPEC],
        out_specs=VMEM_SPEC,
        scratch_shapes=[pltpu.VMEM((inner, 128 + 2 * WIN), jnp.float32)],
        compiler_params=pltpu.CompilerParams(vmem_limit_bytes=VMEM),
        cost_estimate=pl.CostEstimate(
            flops=12 * 10**9, bytes_accessed=6 * 2**20, transcendentals=4 * 10**6
        ),
    )(pos, q, kv)

    after_attn, act = pl.pallas_call(
        middle_kernel,
        out_shape=[
            jax.ShapeDtypeStruct((count, D), jnp.float32),
            jax.ShapeDtypeStruct((count, D), jnp.bfloat16),
        ],
        in_specs=[SMEM_SPEC] + [VMEM_SPEC] * 6 + [ANY_SPEC] * 2,
        out_specs=[VMEM_SPEC, VMEM_SPEC],
        scratch_shapes=[
            pltpu.VMEM((D, WIDTH), jnp.bfloat16),
            pltpu.VMEM((2 * D, D), jnp.bfloat16),
            pltpu.VMEM((2 * PAD, D), jnp.float32),
            pltpu.VMEM((inner, D), jnp.bfloat16),
            pltpu.VMEM((inner, 256), jnp.float32),
            pltpu.VMEM((inner, 256), jnp.float32),
            pltpu.SemaphoreType.DMA((64,)),
        ],
        compiler_params=pltpu.CompilerParams(vmem_limit_bytes=VMEM),
        cost_estimate=pl.CostEstimate(
            flops=20 * 10**9, bytes_accessed=20 * 2**20, transcendentals=2 * 10**6
        ),
    )(
        pos,
        context,
        before,
        rows,
        after,
        conv_gain[None],
        w_depth,
        mid_mine,
        mid_other,
    )
    tail_mine, after_attn, act = lax.optimization_barrier((tail_mine, after_attn, act))
    tail_other = lax.ppermute(tail_mine, BOTH, CORE_SWAP)
    result = pl.pallas_call(
        finish_kernel,
        out_shape=jax.ShapeDtypeStruct((count, D), jnp.bfloat16),
        in_specs=[SMEM_SPEC] + [ANY_SPEC] * 4,
        out_specs=VMEM_SPEC,
        scratch_shapes=[
            pltpu.VMEM((D, D), jnp.bfloat16),
            pltpu.VMEM((count, D), jnp.float32),
            pltpu.VMEM((count, D), jnp.bfloat16),
            pltpu.SemaphoreType.DMA((66,)),
        ],
        compiler_params=pltpu.CompilerParams(vmem_limit_bytes=VMEM),
        cost_estimate=pl.CostEstimate(
            flops=3 * 10**9, bytes_accessed=10 * 2**20, transcendentals=0
        ),
    )(pos, after_attn, act, tail_mine, tail_other)
    return result[None]


def solution(mesh):
    placed = (
        P("stream", "tm", None),
        P("stream"),
        P(),
        P("stream", "tm"),
        P("stream", "tm"),
        P(),
        P("stream", "tm"),
        P(),
        P("stream", "tm"),
    )
    return jax.shard_map(
        shards, mesh=mesh, in_specs=placed, out_specs=P("stream", "tm", None), check_vma=False
    )
```
